32 devices in a mesh: member: 4 (over y, core), region: 8 (over z, x).
Axes of the slice: x: 2, y: 2, z: 4, core: 2. Of those that a mesh axis runs over, the one named last changes fastest.
Arguments:
- latent: bfloat16 [8, 1024, 1024], P('member', 'region'), may hold values from -6 to 6
- w_node: bfloat16 [1024, 1024], replicated, may hold values from -0.1875 to 0.1875
- bias: float32 [1024], replicated, may hold values from -3 to 3
- w_out: bfloat16 [100, 1024], replicated, may hold values from -0.1875 to 0.1875
- edge_src: int32 [16384, 3], P('region'), may hold values from 0 to 383
- edge_weight: float32 [16384, 3], P('region'), may hold values from 0.2 to 0.6
- target: float32 [100, 16384], P(None, 'region'), may hold values from -6 to 6
- area: float32 [16384], P('region'), may hold values from 0.3 to 30
Outputs:
- grad_node: float32 [1024, 1024], P('region')
- grad_out: float32 [100, 1024], replicated
- grad_bias: float32 [1024], replicated
- loss: float32 [8], P('region')
The draws below stay inside these ranges and needn't reach their ends.
Inputs may be any that keep to these rules, and one draw needn't show every extreme that they name: `edge_src`: an index into the latent nodes of the previous region, then the grid point's own region, then the next region, 128 each; regions form a loop.
All inputs are finite; a program needn't handle non-finite values.
Results may differ from the reference program's by a relative error of at most 0.007.
Values may be sent and summed in bfloat16 or wider, within the bound.
A program may use at most 128 MiB of HBM per device.

```python
import jax
import jax.numpy as jnp
from jax import lax

H = 1024
V = 100
K = 3
LAT_DEV = 128
GRID_DEV = 2048
MEMBERS = 8
NLAT = 1024
NGRID = 16384
N_REGION = 8


def draw_area(key, part):
    position = jnp.arange(NGRID).astype(jnp.float32) / NGRID
    spread = jax.random.uniform(key, (NGRID,), jnp.float32, -1.15, 1.15)
    rise = 1.0 + 2.0 * position
    return rise * jnp.exp(spread)


def place_ends(array, stream_key, least, high):
    place = [jax.random.randint(jax.random.fold_in(stream_key, axis), (), 0, length) for axis, length in enumerate(array.shape)]
    longest = array.shape.index(max(array.shape))
    beside = place[:longest] + [(place[longest] + 1) % array.shape[longest]] + place[longest + 1:]
    return array.at[tuple(place)].set(least).at[tuple(beside)].set(high)


def steps_of(stream_key, shape, shards, smallest, high):
    def one(dim, parts):
        steps = jax.random.uniform(jax.random.fold_in(jax.random.fold_in(stream_key, 6), dim), (parts,), jnp.float32, smallest / len(shards), high / len(shards))
        return jnp.repeat(jnp.exp(steps), shape[dim] // parts).reshape((-1,) + (1,) * (len(shape) - dim - 1))

    gain = one(*shards[0])
    for cut in shards[1:]:
        gain = gain * one(*cut)
    return gain


def gaussian(key, shape, scale, reach, split=(), held_as=jnp.bfloat16):
    drawn = jax.random.normal(key, shape, jnp.float32) * scale
    if len(split) > 0:
        drawn = steps_of(key, shape, split, -0.22, 0.18) * drawn
    return jnp.clip(drawn, min=-reach, max=reach).astype(held_as)


def setup_inputs(seed: int = 0) -> dict:
    splits = jax.random.split(jax.random.key(seed), 9)
    latent = gaussian(splits[0], (MEMBERS, NLAT, H), 1.0, 6.0, ((0, 4), (1, 8)))
    w_node = gaussian(splits[1], (H, H), H ** -0.5, 0.1875)
    bias = gaussian(splits[2], (H,), 0.5, 3.0, (), jnp.float32)
    w_out = gaussian(splits[3], (V, H), H ** -0.5, 0.1875)
    edge_src = place_ends(jax.random.randint(splits[4], (NGRID, K), 0, 3 * LAT_DEV), jax.random.fold_in(splits[4], 1), 0, (3 * LAT_DEV) - 1).astype(jnp.int32)
    edge_weight = jnp.clip(0.2 + 0.400000021 * jax.random.uniform(splits[5], (NGRID, K), jnp.float32) ** steps_of(splits[5], (NGRID, K), ((0, 8),), -0.2, 0.2), 0.2, 0.6)
    target = gaussian(splits[6], (V, NGRID), 1.0, 6.0, ((1, 8),), jnp.float32)
    area = draw_area(jax.random.fold_in(splits[8], 71), 0)
    return {"latent": latent, "w_node": w_node, "bias": bias, "w_out": w_out, "edge_src": edge_src, "edge_weight": edge_weight, "target": target, "area": area}


smooth_sq = 0.01
smooth_width = 0.1

def gelu_slope(values):
    inner = 0.7978845608028654 * (values + 0.044715 * values * values * values)
    tanh_part = jnp.tanh(inner)
    return 0.5 * (1.0 + tanh_part) + 0.5 * values * (1.0 - tanh_part * tanh_part) * 0.7978845608028654 * (1.0 + 3.0 * 0.044715 * values * values)

def reference(latent, w_node, bias, w_out, edge_src, edge_weight, target, area):
    grid_region = (jnp.arange(NGRID, dtype=jnp.int32) // GRID_DEV)[:, None]
    node_index = ((grid_region - 1 + edge_src // LAT_DEV) % N_REGION * LAT_DEV + edge_src % LAT_DEV).astype(jnp.int32)
    segment_ids = (grid_region * (3 * LAT_DEV) + edge_src).astype(jnp.int32)
    count = MEMBERS

    def forward(member_latent):
        proj = jnp.dot(member_latent, w_node, preferred_element_type=jnp.float32).astype(jnp.bfloat16)
        pre = jnp.zeros((NGRID, H), jnp.float32) + bias[None, :]
        for slot in range(K):
            pre = pre + edge_weight[:, slot][:, None] * proj[node_index[:, slot]].astype(jnp.float32)
        return pre

    def predict(member_latent):
        hidden = jax.nn.gelu(forward(member_latent), approximate=True).astype(jnp.bfloat16)
        return lax.dot_general(w_out, hidden, (((1,), (1,)), ((), ())), preferred_element_type=jnp.float32)
    preds = lax.map(predict, latent)
    errors = preds - target[None]
    own = jnp.sqrt(errors * errors + smooth_sq)
    dist_sum = jnp.zeros_like(errors)
    slope_sum = jnp.zeros_like(errors)
    for other in range(count):
        diff = errors - errors[other][None]
        dist = jnp.sqrt(diff * diff + smooth_sq)
        dist_sum = dist_sum + dist
        slope_sum = slope_sum + diff / dist
    crps = lax.optimization_barrier(jnp.mean(own, 0)) - (lax.optimization_barrier(jnp.sum(dist_sum, 0)) - count * smooth_width) / (2.0 * count * (count - 1))
    weighted = (area[None, :] * crps).reshape(V, N_REGION, GRID_DEV)
    loss = lax.optimization_barrier(jnp.sum(weighted, axis=(0, 2))) / V / GRID_DEV
    bracket = errors / own / count - slope_sum / (count * (count - 1))
    dpred = (bracket * (area / V)[None, None, :]).astype(jnp.bfloat16)

    def step(carry, pair):
        grad_node, grad_out, grad_bias = carry
        member_latent, member_dpred = pair
        pre = forward(member_latent)
        hidden = jax.nn.gelu(pre, approximate=True).astype(jnp.bfloat16)
        grad_out = grad_out + jnp.dot(member_dpred, hidden, preferred_element_type=jnp.float32)
        dhidden = lax.dot_general(member_dpred, w_out, (((0,), (0,)), ((), ())), preferred_element_type=jnp.float32)
        dpre = (dhidden * gelu_slope(pre)).astype(jnp.bfloat16)
        grad_bias = grad_bias + lax.optimization_barrier(jnp.sum(dpre.astype(jnp.float32), 0))
        contrib = jnp.zeros((N_REGION * 3 * LAT_DEV, H), jnp.float32)
        for slot in range(K):
            contrib = contrib + jax.ops.segment_sum(dpre.astype(jnp.float32) * edge_weight[:, slot][:, None], segment_ids[:, slot], num_segments=N_REGION * 3 * LAT_DEV)
        rounded = contrib.astype(jnp.bfloat16)
        blocks = member_latent.reshape(N_REGION, LAT_DEV, H)
        extended = jnp.stack([jnp.roll(blocks, 1, axis=0), blocks, jnp.roll(blocks, -1, axis=0)], axis=1).reshape(N_REGION * 3 * LAT_DEV, H)
        grad_node = grad_node + lax.dot_general(extended, rounded, (((0,), (0,)), ((), ())), preferred_element_type=jnp.float32)
        return ((grad_node, grad_out, grad_bias), None)
    init = (jnp.zeros((H, H), jnp.float32), jnp.zeros((V, H), jnp.float32), jnp.zeros((H,), jnp.float32))
    (grad_node, grad_out, grad_bias), unused = lax.scan(step, init, (latent, dpred))
    return (grad_node, grad_out, grad_bias, loss)
```

```python
import functools

import jax
import jax.numpy as jnp
from jax import lax
from jax.experimental import pallas as pl
from jax.experimental.pallas import tpu as pltpu
from jax.sharding import PartitionSpec as P

smooth_sq = 0.01
gelu_c = 0.7978845608028654
gelu_a = 0.044715
MESH = pl.DeviceIdType.MESH
BF = jnp.bfloat16
F32 = jnp.float32


def decoder(
    n_member, n_region, variables,
    latent, w_node, bias, w_out, src, weight, src_t, weight_t, target, area,
    grad_node, head_out, loss_out,
    ext, proj, adj, adj_t, hid, slope, preds, dpr, acc, gout, lacc, cb,
    part, recv_c, sum_c, recv_y, sum_y, recv_x, sum_x, recv_z, ob, lbuf,
    halo_s, halo_r, relay_s, relay_r, pa_s, pa_r, pb_s, pb_r, pf_s, pf_r,
    red_s, red_r, z_s, z_r, h_s, h_r, o_s, o_r, l_s, l_r,
):
    here, nodes, width = latent.shape
    points, fanout = src.shape
    span = 3 * nodes
    vp = w_out.shape[0]
    chunks, wide, gc = adj_t.shape
    rb = width // n_region
    quarter = width // 4
    half_n = n_region // 2
    count = here * n_member
    m = lax.axis_index("member")
    r = lax.axis_index("region")
    core = m % 2
    yy = m // 2
    xx = r % 2
    zz = r // 2
    m_core = m + 1 - 2 * core
    m_y = (1 - yy) * 2 + core
    m_diag = (1 - yy) * 2 + 1 - core
    r_x = r + 1 - 2 * xx
    r_relay = (r + n_region + 2 - 4 * xx) % n_region

    def remote(a, b, s, t, mm, rr):
        return pltpu.make_async_remote_copy(
            src_ref=a, dst_ref=b, send_sem=s, recv_sem=t, device_id=(mm, rr), device_id_type=MESH
        )

    barrier = pltpu.get_barrier_semaphore()
    for mm in (m_core, m_y, m_diag):
        pl.semaphore_signal(barrier, inc=1, device_id=(mm, r), device_id_type=MESH)
    for k in range(1, n_region):
        pl.semaphore_signal(
            barrier, inc=1, device_id=(m, (r + k) % n_region), device_id_type=MESH
        )
    pl.semaphore_wait(barrier, n_region + 2)

    far = 2 * xx
    near = 2 - far
    pieces = [(a, b) for a in range(here) for b in range(2)]
    hn = nodes // 2

    def halo(i):
        a, b = pieces[i]
        rows = pl.ds(b * hn, hn)
        return remote(
            latent.at[a, rows], ext.at[far, a, rows], halo_s.at[i], halo_r.at[i], m, r_x
        )

    def relay(i):
        a, b = pieces[i]
        rows = pl.ds(b * hn, hn)
        return remote(
            ext.at[near, a, rows], ext.at[far, a, rows], relay_s.at[i], relay_r.at[i], m, r_relay
        )

    for i in range(len(pieces)):
        halo(i).start()

    def project(slot, x):
        y = jnp.dot(
            x.reshape(here * nodes, width), w_node[...], preferred_element_type=F32
        ).astype(BF)
        for a in range(here):
            proj[a, pl.ds(pl.multiple_of(slot * nodes, nodes), nodes), :] = y[
                a * nodes : (a + 1) * nodes
            ]

    ext[1] = latent[...]
    project(1, latent[...])

    per = chunks // len(pieces)

    def build(c, _):
        rows = pl.ds(pl.multiple_of(c * gc, gc), gc)
        lane = lax.broadcasted_iota(jnp.int32, (gc, span), 1)
        row = lax.broadcasted_iota(jnp.int32, (span, gc), 0)
        s = src[rows, :]
        w = weight[rows, :]
        st = src_t[:, rows]
        wt = weight_t[:, rows]
        a = jnp.zeros((gc, span), F32)
        at = jnp.zeros((span, gc), F32)
        for k in range(fanout):
            a = a + jnp.where(s[:, k : k + 1] == lane, w[:, k : k + 1], 0.0)
            at = at + jnp.where(st[k : k + 1, :] == row, wt[k : k + 1, :], 0.0)
        adj[rows, :] = a.astype(BF)
        adj_t[c, 0:span, :] = at.astype(BF)
        adj_t[c, span:wide, :] = jnp.ones((wide - span, gc), BF)
        return 0

    for i in range(len(pieces)):
        lax.fori_loop(i * per, (i + 1) * per, build, 0)
        halo(i).wait_recv()
        relay(i).start()
    project(near, ext[near])
    for i in range(len(pieces)):
        relay(i).wait_recv()
    project(far, ext[far])

    lag = chunks // 2

    def to_core(c):
        return remote(preds.at[0, c], preds.at[1, c], pa_s.at[c], pa_r.at[c], m_core, r)

    def to_y(c):
        return remote(preds.at[0, c], preds.at[2, c], pb_s.at[c], pb_r.at[c], m_y, r)

    def pass_on(c):
        return remote(preds.at[2, c], preds.at[3, c], pf_s.at[c], pf_r.at[c], m_core, r)

    def forward(c, _):
        rows = pl.ds(pl.multiple_of(c * gc, gc), gc)
        for a in range(here):
            x = jnp.dot(adj[rows, :], proj[a], preferred_element_type=F32) + bias[...]
            u = x * x
            t = jnp.tanh(x * (gelu_c + gelu_c * gelu_a * u))
            p = 0.5 + 0.5 * t
            h = x * p
            hb = h.astype(BF)
            hid[a, rows, :] = hb
            sl = p + h * (1.0 - p) * (2.0 * gelu_c + 6.0 * gelu_c * gelu_a * u)
            slope[a, rows, :] = sl.astype(BF)
            preds[0, c, a] = lax.dot_general(
                w_out[...], hb, (((1,), (1,)), ((), ())), preferred_element_type=F32
            ).astype(BF)
        to_core(c).start()
        to_y(c).start()

        @pl.when(c >= lag)
        def _():
            to_y(c - lag).wait_recv()
            pass_on(c - lag).start()

        return 0

    lax.fori_loop(0, chunks, forward, 0)

    acc[...] = jnp.zeros_like(acc)
    gout[...] = jnp.zeros_like(gout)
    lacc[...] = jnp.zeros_like(lacc)
    step = 16

    def backward(c, _):
        rows = pl.ds(pl.multiple_of(c * gc, gc), gc)

        @pl.when(c < chunks - lag)
        def _():
            to_y(c + lag).wait_recv()
            pass_on(c + lag).start()

        to_core(c).wait_recv()
        pass_on(c).wait_recv()
        arow = area[:, rows]
        ascale = arow * (1.0 / variables)
        for v in range(0, vp, step):
            vs = slice(v, v + step)
            ps = [preds[s, c, a, vs, :].astype(F32) for s in range(4) for a in range(here)]
            tg = target[vs, rows]
            dist = jnp.zeros((step, gc), F32)
            sums = [jnp.zeros((step, gc), F32) for _ in range(here)]
            for a in range(here):
                for b in range(a + 1, count):
                    d = ps[a] - ps[b]
                    q = d * d + smooth_sq
                    i = lax.rsqrt(q)
                    g = d * i
                    sums[a] = sums[a] + g
                    s = q * i
                    if b < here:
                        sums[b] = sums[b] - g
                        s = s + s
                    dist = dist + s
            total = dist * (-1.0 / (2.0 * count * (count - 1)))
            for a in range(here):
                e = ps[a] - tg
                q = e * e + smooth_sq
                i = lax.rsqrt(q)
                total = total + q * i * (1.0 / count)
                br = e * i * (1.0 / count) - sums[a] * (1.0 / (count * (count - 1)))
                dpr[a, vs, :] = (br * ascale).astype(BF)
            total = total * arow
            if v + step > variables:
                keep = lax.broadcasted_iota(jnp.int32, (step, gc), 0) < variables - v
                total = jnp.where(keep, total, 0.0)
            lacc[...] += total
        for a in range(here):
            dp = dpr[a]
            hb = hid[a, rows, :]
            gout[0:vp] += jnp.dot(dp, hb, preferred_element_type=F32)
            dh = lax.dot_general(
                dp, w_out[...], (((0,), (0,)), ((), ())), preferred_element_type=F32
            )
            dpre = (dh * slope[a, rows, :].astype(F32)).astype(BF)
            acc[a] += jnp.dot(adj_t[c], dpre, preferred_element_type=F32)
        return 0

    lax.fori_loop(0, chunks, backward, 0)

    lbuf[0] = jnp.broadcast_to(
        jnp.sum(lacc[...]) * (1.0 / (variables * points)), lbuf.shape[1:]
    )

    def share_loss(k, mm):
        return remote(lbuf.at[0], lbuf.at[k], l_s.at[k - 1], l_r.at[k - 1], mm, r)

    sharing = [share_loss(k + 1, mm) for k, mm in enumerate((m_core, m_y, m_diag))]
    for copy in sharing:
        copy.start()

    bias_row = acc[0, span : span + 1, :]
    for a in range(1, here):
        bias_row = bias_row + acc[a, span : span + 1, :]
    gout[vp : vp + 1] = bias_row
    for a in range(here):
        for s in range(3):
            cb[s, a] = acc[a, s * nodes : (s + 1) * nodes, :].astype(BF)

    tall = 256
    for i in range(0, width, tall):
        left = ext[:, :, :, i : i + tall].reshape(span * here, tall)
        g = lax.dot_general(
            left, cb[...].reshape(span * here, width), (((0,), (0,)), ((), ())),
            preferred_element_type=F32,
        ).astype(BF)
        for j in range(tall // rb):
            q = i // rb + j
            for k in range(4):
                part[k // 2, k % 2, q % 2, q // 2, 0:rb, :] = g[
                    j * rb : (j + 1) * rb, k * quarter : (k + 1) * quarter
                ]
    for q in range(n_region):
        hv = gout[16 * q : 16 * q + 16, :].astype(BF)
        for k in range(4):
            part[k // 2, k % 2, q % 2, q // 2, rb : rb + 16, :] = hv[
                :, k * quarter : (k + 1) * quarter
            ]

    def add(a, b):
        return a.astype(F32) + b.astype(F32)

    c_copy = remote(part.at[1 - core], recv_c, red_s.at[0], red_r.at[0], m_core, r)
    c_copy.start()
    c_copy.wait_recv()

    def add_c(i, _):
        for k in range(2):
            for j in range(2):
                sum_c[k, j, i] = add(part[core, k, j, i], recv_c[k, j, i]).astype(BF)
        return 0

    lax.fori_loop(0, half_n, add_c, 0)
    y_copy = remote(sum_c.at[1 - yy], recv_y, red_s.at[1], red_r.at[1], m_y, r)
    y_copy.start()
    y_copy.wait_recv()

    def add_y(i, _):
        for j in range(2):
            sum_y[j, i] = add(sum_c[yy, j, i], recv_y[j, i]).astype(BF)
        return 0

    lax.fori_loop(0, half_n, add_y, 0)
    x_copy = remote(sum_y.at[1 - xx], recv_x, red_s.at[2], red_r.at[2], m, r_x)
    x_copy.start()
    x_copy.wait_recv()

    def add_x(i, _):
        sum_x[i] = add(sum_y[xx, i], recv_x[i]).astype(BF)
        return 0

    lax.fori_loop(0, half_n, add_x, 0)
    z_copies = []
    for k in range(1, half_n):
        z_to = (zz + k) % half_n
        z_copies.append(
            remote(
                sum_x.at[z_to], recv_z.at[k - 1], z_s.at[k - 1], z_r.at[k - 1], m, 2 * z_to + xx
            )
        )
    for copy in z_copies:
        copy.start()
    total = sum_x[zz].astype(F32)
    for k in range(1, half_n):
        z_copies[k - 1].wait_recv()
        total = total + recv_z[k - 1].astype(F32)
    ob[0, 0:rb, :] = total[0:rb]
    mine = pl.ds(pl.multiple_of(rb + 16 * r, 16), 16)
    ob[0, mine, :] = total[rb : rb + 16]
    h_copies = [
        remote(
            ob.at[0, mine], ob.at[0, mine], h_s.at[k - 1], h_r.at[k - 1], m, (r + k) % n_region
        )
        for k in range(1, n_region)
    ]
    for copy in h_copies:
        copy.start()
    for copy in h_copies:
        copy.wait_recv()
    o_core = remote(ob.at[0], ob.at[1], o_s.at[0], o_r.at[0], m_core, r)
    o_y = remote(ob.at[0], ob.at[2], o_s.at[1], o_r.at[1], m_y, r)
    o_pass = remote(ob.at[2], ob.at[3], o_s.at[2], o_r.at[2], m_core, r)
    o_y.start()
    o_core.start()

    def place(k, mm):
        at = pl.ds(pl.multiple_of(((mm % 2) * 2 + mm // 2) * quarter, quarter), quarter)
        grad_node[:, at] = ob[k, 0:rb, :]
        head_out[:, at] = ob[k, rb:, :]

    place(0, m)
    lsum = lbuf[0]
    for k, copy in enumerate(sharing):
        copy.wait_recv()
        lsum = lsum + lbuf[k + 1]
    loss_out[...] = lsum
    o_core.wait_recv()
    place(1, m_core)
    o_y.wait_recv()
    o_pass.start()
    place(2, m_y)
    o_pass.wait_recv()
    place(3, m_diag)

    for i in range(len(pieces)):
        halo(i).wait_send()
        relay(i).wait_send()

    def drain(c, _):
        to_core(c).wait_send()
        to_y(c).wait_send()
        pass_on(c).wait_send()
        return 0

    lax.fori_loop(0, chunks, drain, 0)
    for copy in [c_copy, y_copy, x_copy, o_core, o_y, o_pass] + z_copies + h_copies + sharing:
        copy.wait_send()


def local(n_member, n_region, latent, w_node, bias, w_out, edge_src, edge_weight, target, area):
    here, nodes, width = latent.shape
    points, fanout = edge_src.shape
    variables = target.shape[0]
    vp = -(-variables // 16) * 16
    gc = 256
    chunks = points // gc
    span = 3 * nodes
    wide = span + 16
    rb = width // n_region
    head = 16 * n_region
    quarter = width // 4
    half_n = n_region // 2
    blk = rb + 16
    grow = max(head, vp + 16)
    dma = lambda k: pltpu.SemaphoreType.DMA((k,))
    vm = lambda shape, t: pltpu.VMEM(shape, t)
    grad_node, heads, loss = pl.pallas_call(
        functools.partial(decoder, n_member, n_region, variables),
        out_shape=(
            jax.ShapeDtypeStruct((rb, width), F32),
            jax.ShapeDtypeStruct((head, width), F32),
            jax.ShapeDtypeStruct((8, 128), F32),
        ),
        in_specs=[pl.BlockSpec(memory_space=pltpu.VMEM)] * 10,
        out_specs=[pl.BlockSpec(memory_space=pltpu.VMEM)] * 3,
        scratch_shapes=[
            vm((3, here, nodes, width), BF),
            vm((here, span, width), BF),
            vm((points, span), BF),
            vm((chunks, wide, gc), BF),
            vm((here, points, width), BF),
            vm((here, points, width), BF),
            vm((4, chunks, here, vp, gc), BF),
            vm((here, vp, gc), BF),
            vm((here, wide, width), F32),
            vm((grow, width), F32),
            vm((16, gc), F32),
            vm((3, here, nodes, width), BF),
            vm((2, 2, 2, half_n, blk, quarter), BF),
            vm((2, 2, half_n, blk, quarter), BF),
            vm((2, 2, half_n, blk, quarter), BF),
            vm((2, half_n, blk, quarter), BF),
            vm((2, half_n, blk, quarter), BF),
            vm((half_n, blk, quarter), BF),
            vm((half_n, blk, quarter), BF),
            vm((half_n - 1, blk, quarter), BF),
            vm((4, rb + head, quarter), F32),
            vm((4, 8, 128), F32),
            dma(4), dma(4), dma(4), dma(4),
            dma(chunks), dma(chunks), dma(chunks), dma(chunks), dma(chunks), dma(chunks),
            dma(3), dma(3), dma(half_n - 1), dma(half_n - 1),
            dma(n_region - 1), dma(n_region - 1), dma(3), dma(3), dma(3), dma(3),
        ],
        compiler_params=pltpu.CompilerParams(
            collective_id=0, has_side_effects=True, vmem_limit_bytes=60 * 2**20
        ),
    )(
        latent, w_node, bias.reshape(1, width),
        jnp.pad(w_out, ((0, vp - variables), (0, 0))),
        edge_src, edge_weight, edge_src.T, edge_weight.T,
        jnp.pad(target, ((0, vp - variables), (0, 0))), area.reshape(1, points),
    )
    return (grad_node, heads[:variables], heads[vp], loss[0, 0:1])


def solution(mesh):
    return jax.shard_map(
        functools.partial(local, mesh.shape["member"], mesh.shape["region"]),
        mesh=mesh,
        in_specs=(
            P("member", "region", None),
            P(),
            P(),
            P(),
            P("region", None),
            P("region", None),
            P(None, "region"),
            P("region"),
        ),
        out_specs=(P("region", None), P(), P(), P("region")),
        check_vma=False,
    )
```

```python
import functools

import jax
import jax.numpy as jnp
from jax import lax
from jax.experimental import pallas as pl
from jax.experimental.pallas import tpu as pltpu
from jax.sharding import PartitionSpec as P

smooth_sq = 0.01
gelu_c = 0.7978845608028654
gelu_a = 0.044715
MESH = pl.DeviceIdType.MESH
BF = jnp.bfloat16
F32 = jnp.float32


def decoder(
    n_member, n_region, variables,
    latent, w_node, bias, w_out_in, src_t, weight_t, target, area,
    grad_node, grad_out, grad_bias, loss_out,
    w_out, tail, ext, proj, adj, adj_t, hid, slope, preds, dpr, acc, gout, lacc, cb,
    part, recv_c, sum_c, recv_1a, recv_1b, sum_1a, sum_1b, recv_2, sum_2, recv_z, ob, lbuf,
    halo_s, halo_r, relay_s, relay_r, pa_s, pa_r, pb_s, pb_r, pf_s, pf_r,
    c_s, c_r, red_s, red_r, z_s, z_r, h_s, h_r, o_s, o_r, l_s, l_r,
):
    here, nodes, width = latent.shape
    fanout, points = src_t.shape
    span = 3 * nodes
    vp = w_out.shape[0]
    chunks, wide, gc = adj_t.shape
    rb = width // n_region
    quarter = width // 4
    half_n = n_region // 2
    count = here * n_member
    m = lax.axis_index("member")
    r = lax.axis_index("region")
    core = m % 2
    yy = m // 2
    xx = r % 2
    zz = r // 2
    m_core = m + 1 - 2 * core
    m_y = (1 - yy) * 2 + core
    m_diag = (1 - yy) * 2 + 1 - core
    r_x = r + 1 - 2 * xx
    r_relay = (r + n_region + 2 - 4 * xx) % n_region

    def remote(a, b, s, t, mm, rr):
        return pltpu.make_async_remote_copy(
            src_ref=a, dst_ref=b, send_sem=s, recv_sem=t, device_id=(mm, rr), device_id_type=MESH
        )

    barrier = pltpu.get_barrier_semaphore()
    for mm in (m_core, m_y, m_diag):
        pl.semaphore_signal(barrier, inc=1, device_id=(mm, r), device_id_type=MESH)
    for k in range(1, n_region):
        pl.semaphore_signal(
            barrier, inc=1, device_id=(m, (r + k) % n_region), device_id_type=MESH
        )
    pl.semaphore_wait(barrier, n_region + 2)

    far = 2 * xx
    near = 2 - far
    pieces = [(a, b) for a in range(here) for b in range(2)]
    hn = nodes // 2

    def halo(i):
        a, b = pieces[i]
        rows = pl.ds(b * hn, hn)
        return remote(
            latent.at[a, rows], ext.at[far, a, rows], halo_s.at[i], halo_r.at[i], m, r_x
        )

    def relay(i):
        a, b = pieces[i]
        rows = pl.ds(b * hn, hn)
        return remote(
            ext.at[near, a, rows], ext.at[far, a, rows], relay_s.at[i], relay_r.at[i], m, r_relay
        )

    for i in range(len(pieces)):
        halo(i).start()

    def project(a):
        proj[a] = jnp.dot(
            ext[:, a].reshape(span, width), w_node[...], preferred_element_type=F32
        ).astype(BF)

    ext[1] = latent[...]
    w_out[0:variables] = w_out_in[...]
    w_out[variables:vp] = jnp.zeros((vp - variables, width), BF)
    tail[...] = jnp.zeros_like(tail)
    tail[0 : variables - (vp - 16)] = target[vp - 16 : variables]

    def build(c, _):
        rows = pl.ds(pl.multiple_of(c * gc, gc), gc)
        row = lax.broadcasted_iota(jnp.int32, (span, gc), 0)
        st = src_t[:, rows]
        wt = weight_t[:, rows]
        at = jnp.zeros((span, gc), F32)
        for k in range(fanout):
            at = at + jnp.where(st[k : k + 1, :] == row, wt[k : k + 1, :], 0.0)
        adj[rows, :] = at.T.astype(BF)
        adj_t[c, 0:span, :] = at.astype(BF)
        adj_t[c, span:wide, :] = jnp.ones((wide - span, gc), BF)
        return 0

    lax.fori_loop(0, chunks // 4, build, 0)
    halo(0).wait_recv()
    relay(0).start()
    lax.fori_loop(chunks // 4, chunks, build, 0)
    halo(1).wait_recv()
    relay(1).start()
    relay(0).wait_recv()
    relay(1).wait_recv()

    lag = chunks // 2

    def blocks(t):
        return t // chunks, t % chunks

    def to_core(t):
        a, c = blocks(t)
        return remote(preds.at[0, a, c], preds.at[1, a, c], pa_s.at[t], pa_r.at[t], m_core, r)

    def to_y(t):
        a, c = blocks(t)
        return remote(preds.at[0, a, c], preds.at[2, a, c], pb_s.at[t], pb_r.at[t], m_y, r)

    def pass_on(t):
        a, c = blocks(t)
        return remote(preds.at[2, a, c], preds.at[3, a, c], pf_s.at[t], pf_r.at[t], m_core, r)

    steps = here * chunks

    def forward(a, c):
        rows = pl.ds(pl.multiple_of(c * gc, gc), gc)
        t = a * chunks + c
        x = jnp.dot(adj[rows, :], proj[a], preferred_element_type=F32) + bias[...]
        u = x * x
        th = jnp.tanh(x * (gelu_c + gelu_c * gelu_a * u))
        p = 0.5 + 0.5 * th
        h = x * p
        hb = h.astype(BF)
        hid[a, rows, :] = hb
        sl = p + h * (1.0 - p) * (2.0 * gelu_c + 6.0 * gelu_c * gelu_a * u)
        slope[a, rows, :] = sl.astype(BF)
        preds[0, a, c] = lax.dot_general(
            w_out[...], hb, (((1,), (1,)), ((), ())), preferred_element_type=F32
        ).astype(BF)
        to_y(t).start()
        to_core(t).start()

        @pl.when(t >= lag)
        def _():
            to_y(t - lag).wait_recv()
            pass_on(t - lag).start()

    for a in range(here):
        project(a)

        def run(c, _):
            if a + 1 < here:
                for b in range(2):
                    @pl.when(c == 2 * b)
                    def _():
                        halo(2 * a + 2 + b).wait_recv()
                        relay(2 * a + 2 + b).start()

            forward(a, c)
            return 0

        lax.fori_loop(0, chunks, run, 0)
        if a + 1 < here:
            for b in range(2):
                relay(2 * a + 2 + b).wait_recv()

    acc[...] = jnp.zeros_like(acc)
    gout[...] = jnp.zeros_like(gout)
    lacc[...] = jnp.zeros_like(lacc)
    step = 16

    def backward(c, _):
        rows = pl.ds(pl.multiple_of(c * gc, gc), gc)

        @pl.when(c < lag)
        def _():
            to_y(steps - lag + c).wait_recv()
            pass_on(steps - lag + c).start()

        for a in range(here):
            to_core(a * chunks + c).wait_recv()
            pass_on(a * chunks + c).wait_recv()
        arow = area[:, rows]
        ascale = arow * (1.0 / variables)
        for v in range(0, vp, step):
            vs = slice(v, v + step)
            ps = [preds[s, a, c, vs, :].astype(F32) for s in range(4) for a in range(here)]
            tg = target[vs, rows] if v + step <= variables else tail[:, rows]
            dist = jnp.zeros((step, gc), F32)
            sums = [jnp.zeros((step, gc), F32) for _ in range(here)]
            for a in range(here):
                for b in range(a + 1, count):
                    d = ps[a] - ps[b]
                    q = d * d + smooth_sq
                    i = lax.rsqrt(q)
                    g = d * i
                    sums[a] = sums[a] + g
                    s = q * i
                    if b < here:
                        sums[b] = sums[b] - g
                        s = s + s
                    dist = dist + s
            total = dist * (-1.0 / (2.0 * count * (count - 1)))
            for a in range(here):
                e = ps[a] - tg
                q = e * e + smooth_sq
                i = lax.rsqrt(q)
                total = total + q * i * (1.0 / count)
                br = e * i * (1.0 / count) - sums[a] * (1.0 / (count * (count - 1)))
                dpr[a, vs, :] = (br * ascale).astype(BF)
            total = total * arow
            if v + step > variables:
                keep = lax.broadcasted_iota(jnp.int32, (step, gc), 0) < variables - v
                total = jnp.where(keep, total, 0.0)
            lacc[...] += total
        for a in range(here):
            dp = dpr[a]
            hb = hid[a, rows, :]
            gout[0:vp] += jnp.dot(dp, hb, preferred_element_type=F32)
            dh = lax.dot_general(
                dp, w_out[...], (((0,), (0,)), ((), ())), preferred_element_type=F32
            )
            dpre = (dh * slope[a, rows, :].astype(F32)).astype(BF)
            acc[a] += jnp.dot(adj_t[c], dpre, preferred_element_type=F32)
        return 0

    lax.fori_loop(0, chunks, backward, 0)

    lbuf[0] = jnp.broadcast_to(
        jnp.sum(lacc[...]) * (1.0 / (variables * points)), lbuf.shape[1:]
    )

    def share_loss(k, mm):
        return remote(lbuf.at[0], lbuf.at[k], l_s.at[k - 1], l_r.at[k - 1], mm, r)

    sharing = [share_loss(k + 1, mm) for k, mm in enumerate((m_core, m_y, m_diag))]
    for copy in sharing:
        copy.start()

    bias_row = acc[0, span : span + 1, :]
    for a in range(1, here):
        bias_row = bias_row + acc[a, span : span + 1, :]
    gout[vp : vp + 1] = bias_row
    for a in range(here):
        for s in range(3):
            cb[s * here + a] = acc[a, s * nodes : (s + 1) * nodes, :].astype(BF)

    def add(a, b):
        return a.astype(F32) + b.astype(F32)

    c_copies = [
        remote(part.at[0, k], recv_c.at[k], c_s.at[k], c_r.at[k], m_core, r) for k in range(2)
    ]
    tall = 256
    lanes = quarter // 2
    for hh, side in enumerate((1 - core, core)):
        cols = pl.ds(pl.multiple_of(side * 2 * quarter, 2 * quarter), 2 * quarter)
        right = cb[:, :, cols].reshape(span * here, 2 * quarter)
        for i in range(0, width, tall):
            left = ext[:, :, :, i : i + tall].reshape(span * here, tall)
            g = lax.dot_general(
                left, right, (((0,), (0,)), ((), ())), preferred_element_type=F32
            ).astype(BF)
            for j in range(tall // rb):
                q = i // rb + j
                for k in range(4):
                    part[hh, k % 2, k // 2, q % 2, q // 2, 0:rb, :] = g[
                        j * rb : (j + 1) * rb, k * lanes : (k + 1) * lanes
                    ]
        for q in range(n_region):
            hv = gout[16 * q : 16 * q + 16, cols].astype(BF)
            for k in range(4):
                part[hh, k % 2, k // 2, q % 2, q // 2, rb : rb + 16, :] = hv[
                    :, k * lanes : (k + 1) * lanes
                ]
        if hh == 0:
            for copy in c_copies:
                copy.start()

    def add_c(k):
        def body(i, _):
            for a in range(2):
                for b in range(2):
                    sum_c[k, a, b, i] = add(part[1, k, a, b, i], recv_c[k, a, b, i]).astype(BF)
            return 0

        lax.fori_loop(0, half_n, body, 0)

    a1 = remote(sum_c.at[0, 1 - yy], recv_1a, red_s.at[0], red_r.at[0], m_y, r)
    b1 = remote(sum_c.at[1, :, 1 - xx], recv_1b, red_s.at[1], red_r.at[1], m, r_x)
    a2 = remote(sum_1a.at[1 - xx], recv_2.at[0], red_s.at[2], red_r.at[2], m, r_x)
    b2 = remote(sum_1b.at[1 - yy], recv_2.at[1], red_s.at[3], red_r.at[3], m_y, r)
    for k, copy in enumerate((a1, b1)):
        c_copies[k].wait_recv()
        add_c(k)
        copy.start()

    def add_1a(i, _):
        for b in range(2):
            sum_1a[b, i] = add(sum_c[0, yy, b, i], recv_1a[b, i]).astype(BF)
        return 0

    def add_1b(i, _):
        for b in range(2):
            sum_1b[b, i] = add(sum_c[1, b, xx, i], recv_1b[b, i]).astype(BF)
        return 0

    a1.wait_recv()
    lax.fori_loop(0, half_n, add_1a, 0)
    a2.start()
    b1.wait_recv()
    lax.fori_loop(0, half_n, add_1b, 0)
    b2.start()

    def add_2a(i, _):
        sum_2[i, 0] = add(sum_1a[xx, i], recv_2[0, i]).astype(BF)
        return 0

    def add_2b(i, _):
        sum_2[i, 1] = add(sum_1b[yy, i], recv_2[1, i]).astype(BF)
        return 0

    a2.wait_recv()
    lax.fori_loop(0, half_n, add_2a, 0)
    b2.wait_recv()
    lax.fori_loop(0, half_n, add_2b, 0)
    z_copies = []
    for k in range(1, half_n):
        z_to = (zz + k) % half_n
        z_copies.append(
            remote(
                sum_2.at[z_to], recv_z.at[k - 1], z_s.at[k - 1], z_r.at[k - 1], m, 2 * z_to + xx
            )
        )
    for copy in z_copies:
        copy.start()
    mine = pl.ds(pl.multiple_of(rb + 16 * r, 16), 16)
    totals = [sum_2[zz, k].astype(F32) for k in range(2)]
    for i in range(1, half_n):
        z_copies[i - 1].wait_recv()
        for k in range(2):
            totals[k] = totals[k] + recv_z[i - 1, k].astype(F32)
    for k in range(2):
        at = slice(k * lanes, (k + 1) * lanes)
        ob[0, 0:rb, at] = totals[k][0:rb].astype(BF)
        ob[0, mine, at] = totals[k][rb : rb + 16].astype(BF)
    h_copies = [
        remote(
            ob.at[0, mine], ob.at[0, mine], h_s.at[k - 1], h_r.at[k - 1], m, (r + k) % n_region
        )
        for k in range(1, n_region)
    ]
    for copy in h_copies:
        copy.start()
    tops, lows = pl.ds(0, rb), pl.ds(rb, 16 * n_region)

    def spread(rows, k):
        one = remote(ob.at[0, rows], ob.at[1, rows], o_s.at[k], o_r.at[k], m_core, r)
        two = remote(ob.at[0, rows], ob.at[2, rows], o_s.at[k + 1], o_r.at[k + 1], m_y, r)
        on = remote(ob.at[2, rows], ob.at[3, rows], o_s.at[k + 2], o_r.at[k + 2], m_core, r)
        return one, two, on

    t_core, t_y, t_on = spread(tops, 0)
    b_core, b_y, b_on = spread(lows, 3)
    t_y.start()
    t_core.start()

    def columns(mm):
        return pl.ds(pl.multiple_of(((mm % 2) * 2 + mm // 2) * quarter, quarter), quarter)

    def place_top(k, mm):
        grad_node[:, columns(mm)] = ob[k, 0:rb, :].astype(F32)

    def place_low(k, mm):
        grad_out[:, columns(mm)] = ob[k, rb : rb + vp, :].astype(F32)[0:variables]
        grad_bias[:, columns(mm)] = ob[k, rb + vp : rb + vp + 16, :].astype(F32)[0:1]

    place_top(0, m)
    for copy in sharing:
        copy.wait_recv()
    loss_out[0] = jnp.max((lbuf[0] + lbuf[1]) + (lbuf[2] + lbuf[3]))
    for copy in h_copies:
        copy.wait_recv()
    b_y.start()
    b_core.start()
    t_y.wait_recv()
    t_on.start()
    place_top(2, m_y)
    t_core.wait_recv()
    place_top(1, m_core)
    place_low(0, m)
    b_y.wait_recv()
    b_on.start()
    place_low(2, m_y)
    b_core.wait_recv()
    place_low(1, m_core)
    t_on.wait_recv()
    place_top(3, m_diag)
    b_on.wait_recv()
    place_low(3, m_diag)

    for i in range(len(pieces)):
        halo(i).wait_send()
        relay(i).wait_send()

    def drain(c, _):
        to_core(c).wait_send()
        to_y(c).wait_send()
        pass_on(c).wait_send()
        return 0

    lax.fori_loop(0, steps, drain, 0)
    ends = [a1, b1, a2, b2, t_core, t_y, t_on, b_core, b_y, b_on]
    for copy in ends + c_copies + z_copies + h_copies + sharing:
        copy.wait_send()


def local(n_member, n_region, latent, w_node, bias, w_out, edge_src, edge_weight, target, area):
    here, nodes, width = latent.shape
    points, fanout = edge_src.shape
    variables = target.shape[0]
    vp = -(-variables // 16) * 16
    gc = 256
    chunks = points // gc
    span = 3 * nodes
    wide = span + 16
    rb = width // n_region
    head = 16 * n_region
    quarter = width // 4
    lanes = quarter // 2
    half_n = n_region // 2
    blk = rb + 16
    grow = max(head, vp + 16)
    dma = lambda k: pltpu.SemaphoreType.DMA((k,))
    vm = lambda shape, t: pltpu.VMEM(shape, t)
    grad_node, grad_out, grad_bias, loss = pl.pallas_call(
        functools.partial(decoder, n_member, n_region, variables),
        out_shape=(
            jax.ShapeDtypeStruct((rb, width), F32),
            jax.ShapeDtypeStruct((variables, width), F32),
            jax.ShapeDtypeStruct((1, width), F32),
            jax.ShapeDtypeStruct((1,), F32),
        ),
        in_specs=[pl.BlockSpec(memory_space=pltpu.VMEM)] * 8,
        out_specs=[pl.BlockSpec(memory_space=pltpu.VMEM)] * 3
        + [pl.BlockSpec(memory_space=pltpu.SMEM)],
        scratch_shapes=[
            vm((vp, width), BF),
            vm((16, points), F32),
            vm((3, here, nodes, width), BF),
            vm((here, span, width), BF),
            vm((points, span), BF),
            vm((chunks, wide, gc), BF),
            vm((here, points, width), BF),
            vm((here, points, width), BF),
            vm((4, here, chunks, vp, gc), BF),
            vm((here, vp, gc), BF),
            vm((here, wide, width), F32),
            vm((grow, width), F32),
            vm((16, gc), F32),
            vm((3 * here, nodes, width), BF),
            vm((2, 2, 2, 2, half_n, blk, lanes), BF),
            vm((2, 2, 2, half_n, blk, lanes), BF),
            vm((2, 2, 2, half_n, blk, lanes), BF),
            vm((2, half_n, blk, lanes), BF),
            vm((2, half_n, blk, lanes), BF),
            vm((2, half_n, blk, lanes), BF),
            vm((2, half_n, blk, lanes), BF),
            vm((2, half_n, blk, lanes), BF),
            vm((half_n, 2, blk, lanes), BF),
            vm((half_n - 1, 2, blk, lanes), BF),
            vm((4, rb + head, quarter), BF),
            vm((4, 8, 128), F32),
            dma(4), dma(4), dma(4), dma(4),
            *[dma(here * chunks) for _ in range(6)],
            dma(2), dma(2), dma(4), dma(4), dma(half_n - 1), dma(half_n - 1),
            dma(n_region - 1), dma(n_region - 1), dma(6), dma(6), dma(3), dma(3),
        ],
        compiler_params=pltpu.CompilerParams(
            collective_id=0, has_side_effects=True, vmem_limit_bytes=60 * 2**20
        ),
    )(
        latent, w_node, bias.reshape(1, width), w_out, edge_src.T, edge_weight.T, target,
        area.reshape(1, points),
    )
    return (grad_node, grad_out, grad_bias.reshape(width), loss)


def solution(mesh):
    return jax.shard_map(
        functools.partial(local, mesh.shape["member"], mesh.shape["region"]),
        mesh=mesh,
        in_specs=(
            P("member", "region", None),
            P(),
            P(),
            P(),
            P("region", None),
            P("region", None),
            P(None, "region"),
            P("region"),
        ),
        out_specs=(P("region", None), P(), P(), P("region")),
        check_vma=False,
    )
```

```python
import functools

import jax
import jax.numpy as jnp
from jax import lax
from jax.experimental import pallas as pl
from jax.experimental.pallas import tpu as pltpu
from jax.sharding import PartitionSpec as P

smooth_sq = 0.01
gelu_c = 0.7978845608028654
gelu_a = 0.044715
MESH = pl.DeviceIdType.MESH
BF = jnp.bfloat16
F32 = jnp.float32


def decoder(
    n_member, n_region, variables,
    latent, w_node, bias, w_out_in, src_t, weight_t, target, area,
    node_out, head_out, loss_out,
    w_out, tail, ext, proj, adj, adj_t, hid, slope, preds, dpr, acc, gout, lacc, cb,
    part, recv_c, sum_c, recv_1a, recv_1b, sum_1a, sum_1b, recv_2, sum_2, recv_z, ob, lbuf,
    halo_s, halo_r, relay_s, relay_r, pa_s, pa_r, pb_s, pb_r, pf_s, pf_r,
    c_s, c_r, red_s, red_r, z_s, z_r, h_s, h_r, o_s, o_r, l_s, l_r,
):
    here, nodes, width = latent.shape
    fanout, points = src_t.shape
    span = 3 * nodes
    vp = w_out.shape[0]
    chunks, wide, gc = adj_t.shape
    rb = width // n_region
    quarter = width // 4
    half_n = n_region // 2
    count = here * n_member
    m = lax.axis_index("member")
    r = lax.axis_index("region")
    core = m % 2
    yy = m // 2
    xx = r % 2
    zz = r // 2
    m_core = m + 1 - 2 * core
    m_y = (1 - yy) * 2 + core
    m_diag = (1 - yy) * 2 + 1 - core
    r_x = r + 1 - 2 * xx
    r_relay = (r + n_region + 2 - 4 * xx) % n_region

    def remote(a, b, s, t, mm, rr):
        return pltpu.make_async_remote_copy(
            src_ref=a, dst_ref=b, send_sem=s, recv_sem=t, device_id=(mm, rr), device_id_type=MESH
        )

    barrier = pltpu.get_barrier_semaphore()
    for mm in (m_core, m_y, m_diag):
        pl.semaphore_signal(barrier, inc=1, device_id=(mm, r), device_id_type=MESH)
    for k in range(1, n_region):
        pl.semaphore_signal(
            barrier, inc=1, device_id=(m, (r + k) % n_region), device_id_type=MESH
        )
    pl.semaphore_wait(barrier, n_region + 2)

    far = 2 * xx
    near = 2 - far
    pieces = [(a, b) for a in range(here) for b in range(2)]
    hn = nodes // 2

    def halo(i):
        a, b = pieces[i]
        rows = pl.ds(b * hn, hn)
        return remote(
            latent.at[a, rows], ext.at[far, a, rows], halo_s.at[i], halo_r.at[i], m, r_x
        )

    def relay(i):
        a, b = pieces[i]
        rows = pl.ds(b * hn, hn)
        return remote(
            ext.at[near, a, rows], ext.at[far, a, rows], relay_s.at[i], relay_r.at[i], m, r_relay
        )

    for i in range(len(pieces)):
        halo(i).start()

    def project(a):
        proj[a] = jnp.dot(
            ext[:, a].reshape(span, width), w_node[...], preferred_element_type=F32
        ).astype(BF)

    ext[1] = latent[...]
    w_out[0:variables] = w_out_in[...]
    w_out[variables:vp] = jnp.zeros((vp - variables, width), BF)
    tail[...] = jnp.zeros_like(tail)
    tail[0 : variables - (vp - 16)] = target[vp - 16 : variables]

    def build(c, _):
        rows = pl.ds(pl.multiple_of(c * gc, gc), gc)
        row = lax.broadcasted_iota(jnp.int32, (span, gc), 0)
        st = src_t[:, rows]
        wt = weight_t[:, rows]
        at = jnp.zeros((span, gc), F32)
        for k in range(fanout):
            at = at + jnp.where(st[k : k + 1, :] == row, wt[k : k + 1, :], 0.0)
        adj[rows, :] = at.T.astype(BF)
        adj_t[c, 0:span, :] = at.astype(BF)
        adj_t[c, span:wide, :] = jnp.ones((wide - span, gc), BF)
        return 0

    lax.fori_loop(0, chunks // 4, build, 0)
    halo(0).wait_recv()
    relay(0).start()
    lax.fori_loop(chunks // 4, chunks, build, 0)
    halo(1).wait_recv()
    relay(1).start()
    relay(0).wait_recv()
    relay(1).wait_recv()

    lag = chunks // 2

    def blocks(t):
        return t // chunks, t % chunks

    def to_core(t):
        a, c = blocks(t)
        return remote(preds.at[0, a, c], preds.at[1, a, c], pa_s.at[t], pa_r.at[t], m_core, r)

    def to_y(t):
        a, c = blocks(t)
        return remote(preds.at[0, a, c], preds.at[2, a, c], pb_s.at[t], pb_r.at[t], m_y, r)

    def pass_on(t):
        a, c = blocks(t)
        return remote(preds.at[2, a, c], preds.at[3, a, c], pf_s.at[t], pf_r.at[t], m_core, r)

    steps = here * chunks

    def forward(a, c):
        rows = pl.ds(pl.multiple_of(c * gc, gc), gc)
        t = a * chunks + c
        x = jnp.dot(adj[rows, :], proj[a], preferred_element_type=F32) + bias[...]
        u = x * x
        th = jnp.tanh(x * (gelu_c + gelu_c * gelu_a * u))
        p = 0.5 + 0.5 * th
        h = x * p
        hb = h.astype(BF)
        hid[a, rows, :] = hb
        sl = p + h * (1.0 - p) * (2.0 * gelu_c + 6.0 * gelu_c * gelu_a * u)
        slope[a, rows, :] = sl.astype(BF)
        preds[0, a, c] = lax.dot_general(
            w_out[...], hb, (((1,), (1,)), ((), ())), preferred_element_type=F32
        ).astype(BF)
        to_y(t).start()
        to_core(t).start()

        @pl.when(t >= lag)
        def _():
            to_y(t - lag).wait_recv()
            pass_on(t - lag).start()

    for a in range(here):
        project(a)

        def run(c, _):
            if a + 1 < here:
                for b in range(2):
                    @pl.when(c == 2 * b)
                    def _():
                        halo(2 * a + 2 + b).wait_recv()
                        relay(2 * a + 2 + b).start()

            forward(a, c)
            return 0

        lax.fori_loop(0, chunks, run, 0)
        if a + 1 < here:
            for b in range(2):
                relay(2 * a + 2 + b).wait_recv()

    acc[...] = jnp.zeros_like(acc)
    gout[...] = jnp.zeros_like(gout)
    lacc[...] = jnp.zeros_like(lacc)
    step = 16

    def backward(c, _):
        rows = pl.ds(pl.multiple_of(c * gc, gc), gc)

        @pl.when(c < lag)
        def _():
            to_y(steps - lag + c).wait_recv()
            pass_on(steps - lag + c).start()

        for a in range(here):
            to_core(a * chunks + c).wait_recv()
            pass_on(a * chunks + c).wait_recv()
        arow = area[:, rows]
        ascale = arow * (1.0 / variables)
        for v in range(0, vp, step):
            vs = slice(v, v + step)
            ps = [preds[s, a, c, vs, :].astype(F32) for s in range(4) for a in range(here)]
            tg = target[vs, rows] if v + step <= variables else tail[:, rows]
            dist = jnp.zeros((step, gc), F32)
            sums = [jnp.zeros((step, gc), F32) for _ in range(here)]
            for a in range(here):
                for b in range(a + 1, count):
                    d = ps[a] - ps[b]
                    q = d * d + smooth_sq
                    i = lax.rsqrt(q)
                    g = d * i
                    sums[a] = sums[a] + g
                    s = q * i
                    if b < here:
                        sums[b] = sums[b] - g
                        s = s + s
                    dist = dist + s
            total = dist * (-1.0 / (2.0 * count * (count - 1)))
            for a in range(here):
                e = ps[a] - tg
                q = e * e + smooth_sq
                i = lax.rsqrt(q)
                total = total + q * i * (1.0 / count)
                br = e * i * (1.0 / count) - sums[a] * (1.0 / (count * (count - 1)))
                dpr[a, vs, :] = (br * ascale).astype(BF)
            total = total * arow
            if v + step > variables:
                keep = lax.broadcasted_iota(jnp.int32, (step, gc), 0) < variables - v
                total = jnp.where(keep, total, 0.0)
            lacc[...] += total
        for a in range(here):
            dp = dpr[a]
            hb = hid[a, rows, :]
            gout[0:vp] += jnp.dot(dp, hb, preferred_element_type=F32)
            dh = lax.dot_general(
                dp, w_out[...], (((0,), (0,)), ((), ())), preferred_element_type=F32
            )
            dpre = (dh * slope[a, rows, :].astype(F32)).astype(BF)
            acc[a] += jnp.dot(adj_t[c], dpre, preferred_element_type=F32)
        return 0

    lax.fori_loop(0, chunks, backward, 0)

    lbuf[0] = jnp.broadcast_to(
        jnp.sum(lacc[...]) * (1.0 / (variables * points)), lbuf.shape[1:]
    )

    def share_loss(k, mm):
        return remote(lbuf.at[0], lbuf.at[k], l_s.at[k - 1], l_r.at[k - 1], mm, r)

    sharing = [share_loss(k + 1, mm) for k, mm in enumerate((m_core, m_y, m_diag))]
    for copy in sharing:
        copy.start()

    bias_row = acc[0, span : span + 1, :]
    for a in range(1, here):
        bias_row = bias_row + acc[a, span : span + 1, :]
    gout[vp : vp + 1] = bias_row
    for a in range(here):
        for s in range(3):
            cb[s * here + a] = acc[a, s * nodes : (s + 1) * nodes, :].astype(BF)

    def add(a, b):
        return a.astype(F32) + b.astype(F32)

    c_copies = [
        remote(part.at[0, k], recv_c.at[k], c_s.at[k], c_r.at[k], m_core, r) for k in range(2)
    ]
    tall = 256
    lanes = quarter // 2
    for hh, side in enumerate((1 - core, core)):
        cols = pl.ds(pl.multiple_of(side * 2 * quarter, 2 * quarter), 2 * quarter)
        right = cb[:, :, cols].reshape(span * here, 2 * quarter)
        for i in range(0, width, tall):
            left = ext[:, :, :, i : i + tall].reshape(span * here, tall)
            g = lax.dot_general(
                left, right, (((0,), (0,)), ((), ())), preferred_element_type=F32
            ).astype(BF)
            for j in range(tall // rb):
                q = i // rb + j
                for k in range(4):
                    part[hh, k % 2, k // 2, q % 2, q // 2, 0:rb, :] = g[
                        j * rb : (j + 1) * rb, k * lanes : (k + 1) * lanes
                    ]
        for q in range(n_region):
            hv = gout[16 * q : 16 * q + 16, cols].astype(BF)
            for k in range(4):
                part[hh, k % 2, k // 2, q % 2, q // 2, rb : rb + 16, :] = hv[
                    :, k * lanes : (k + 1) * lanes
                ]
        if hh == 0:
            for copy in c_copies:
                copy.start()

    def add_c(k):
        def body(i, _):
            for a in range(2):
                for b in range(2):
                    sum_c[k, a, b, i] = add(part[1, k, a, b, i], recv_c[k, a, b, i]).astype(BF)
            return 0

        lax.fori_loop(0, half_n, body, 0)

    a1 = remote(sum_c.at[0, 1 - yy], recv_1a, red_s.at[0], red_r.at[0], m_y, r)
    b1 = remote(sum_c.at[1, :, 1 - xx], recv_1b, red_s.at[1], red_r.at[1], m, r_x)
    a2 = remote(sum_1a.at[1 - xx], recv_2.at[0], red_s.at[2], red_r.at[2], m, r_x)
    b2 = remote(sum_1b.at[1 - yy], recv_2.at[1], red_s.at[3], red_r.at[3], m_y, r)
    for k, copy in enumerate((a1, b1)):
        c_copies[k].wait_recv()
        add_c(k)
        copy.start()

    def add_1a(i, _):
        for b in range(2):
            sum_1a[b, i] = add(sum_c[0, yy, b, i], recv_1a[b, i]).astype(BF)
        return 0

    def add_1b(i, _):
        for b in range(2):
            sum_1b[b, i] = add(sum_c[1, b, xx, i], recv_1b[b, i]).astype(BF)
        return 0

    a1.wait_recv()
    lax.fori_loop(0, half_n, add_1a, 0)
    a2.start()
    b1.wait_recv()
    lax.fori_loop(0, half_n, add_1b, 0)
    b2.start()

    def add_2a(i, _):
        sum_2[i, 0] = add(sum_1a[xx, i], recv_2[0, i]).astype(BF)
        return 0

    def add_2b(i, _):
        sum_2[i, 1] = add(sum_1b[yy, i], recv_2[1, i]).astype(BF)
        return 0

    a2.wait_recv()
    lax.fori_loop(0, half_n, add_2a, 0)
    b2.wait_recv()
    lax.fori_loop(0, half_n, add_2b, 0)
    z_copies = []
    for k in range(1, half_n):
        z_to = (zz + k) % half_n
        z_copies.append(
            remote(
                sum_2.at[z_to], recv_z.at[k - 1], z_s.at[k - 1], z_r.at[k - 1], m, 2 * z_to + xx
            )
        )
    for copy in z_copies:
        copy.start()
    mine = pl.ds(pl.multiple_of(rb + 16 * r, 16), 16)
    totals = [sum_2[zz, k].astype(F32) for k in range(2)]
    for i in range(1, half_n):
        z_copies[i - 1].wait_recv()
        for k in range(2):
            totals[k] = totals[k] + recv_z[i - 1, k].astype(F32)
    for k in range(2):
        at = slice(k * lanes, (k + 1) * lanes)
        ob[0, 0:rb, at] = totals[k][0:rb].astype(BF)
        ob[0, mine, at] = totals[k][rb : rb + 16].astype(BF)
    h_copies = [
        remote(
            ob.at[0, mine], ob.at[0, mine], h_s.at[k - 1], h_r.at[k - 1], m, (r + k) % n_region
        )
        for k in range(1, n_region)
    ]
    for copy in h_copies:
        copy.start()
    tops, lows = pl.ds(0, rb), pl.ds(rb, 16 * n_region)

    def spread(rows, k):
        one = remote(ob.at[0, rows], ob.at[1, rows], o_s.at[k], o_r.at[k], m_core, r)
        two = remote(ob.at[0, rows], ob.at[2, rows], o_s.at[k + 1], o_r.at[k + 1], m_y, r)
        on = remote(ob.at[2, rows], ob.at[3, rows], o_s.at[k + 2], o_r.at[k + 2], m_core, r)
        return one, two, on

    t_core, t_y, t_on = spread(tops, 0)
    b_core, b_y, b_on = spread(lows, 3)
    t_y.start()
    t_core.start()

    def columns(mm):
        return pl.ds(pl.multiple_of(((mm % 2) * 2 + mm // 2) * quarter, quarter), quarter)

    def place_top(k, mm):
        node_out[:, columns(mm)] = ob[k, 0:rb, :]

    def place_low(k, mm):
        head_out[:, columns(mm)] = ob[k, rb : rb + vp + 16, :]

    place_top(0, m)
    for copy in sharing:
        copy.wait_recv()
    loss_out[...] = (lbuf[0] + lbuf[1]) + (lbuf[2] + lbuf[3])
    for copy in h_copies:
        copy.wait_recv()
    b_y.start()
    b_core.start()
    t_y.wait_recv()
    t_on.start()
    place_top(2, m_y)
    t_core.wait_recv()
    place_top(1, m_core)
    place_low(0, m)
    b_y.wait_recv()
    b_on.start()
    place_low(2, m_y)
    b_core.wait_recv()
    place_low(1, m_core)
    t_on.wait_recv()
    place_top(3, m_diag)
    b_on.wait_recv()
    place_low(3, m_diag)

    for i in range(len(pieces)):
        halo(i).wait_send()
        relay(i).wait_send()

    def drain(c, _):
        to_core(c).wait_send()
        to_y(c).wait_send()
        pass_on(c).wait_send()
        return 0

    lax.fori_loop(0, steps, drain, 0)
    ends = [a1, b1, a2, b2, t_core, t_y, t_on, b_core, b_y, b_on]
    for copy in ends + c_copies + z_copies + h_copies + sharing:
        copy.wait_send()


def widen(variables, vp, node_half, head_half, loss_sum, grad_node, grad_out, grad_bias, loss):
    grad_node[...] = node_half[...].astype(F32)
    grad_out[...] = head_half[0:vp, :].astype(F32)[0:variables]
    grad_bias[...] = head_half[vp : vp + 16, :].astype(F32)[0:1]
    loss[0] = jnp.max(loss_sum[...])


def local(n_member, n_region, latent, w_node, bias, w_out, edge_src, edge_weight, target, area):
    here, nodes, width = latent.shape
    points, fanout = edge_src.shape
    variables = target.shape[0]
    vp = -(-variables // 16) * 16
    gc = 512
    chunks = points // gc
    span = 3 * nodes
    wide = span + 16
    rb = width // n_region
    head = 16 * n_region
    quarter = width // 4
    lanes = quarter // 2
    half_n = n_region // 2
    blk = rb + 16
    grow = max(head, vp + 16)
    dma = lambda k: pltpu.SemaphoreType.DMA((k,))
    vm = lambda shape, t: pltpu.VMEM(shape, t)
    node_half, head_half, loss_sum = pl.pallas_call(
        functools.partial(decoder, n_member, n_region, variables),
        out_shape=(
            jax.ShapeDtypeStruct((rb, width), BF),
            jax.ShapeDtypeStruct((vp + 16, width), BF),
            jax.ShapeDtypeStruct((8, 128), F32),
        ),
        in_specs=[pl.BlockSpec(memory_space=pltpu.VMEM)] * 8,
        out_specs=[pl.BlockSpec(memory_space=pltpu.VMEM)] * 3,
        scratch_shapes=[
            vm((vp, width), BF),
            vm((16, points), F32),
            vm((3, here, nodes, width), BF),
            vm((here, span, width), BF),
            vm((points, span), BF),
            vm((chunks, wide, gc), BF),
            vm((here, points, width), BF),
            vm((here, points, width), BF),
            vm((4, here, chunks, vp, gc), BF),
            vm((here, vp, gc), BF),
            vm((here, wide, width), F32),
            vm((grow, width), F32),
            vm((16, gc), F32),
            vm((3 * here, nodes, width), BF),
            vm((2, 2, 2, 2, half_n, blk, lanes), BF),
            vm((2, 2, 2, half_n, blk, lanes), BF),
            vm((2, 2, 2, half_n, blk, lanes), BF),
            vm((2, half_n, blk, lanes), BF),
            vm((2, half_n, blk, lanes), BF),
            vm((2, half_n, blk, lanes), BF),
            vm((2, half_n, blk, lanes), BF),
            vm((2, half_n, blk, lanes), BF),
            vm((half_n, 2, blk, lanes), BF),
            vm((half_n - 1, 2, blk, lanes), BF),
            vm((4, rb + head, quarter), BF),
            vm((4, 8, 128), F32),
            dma(4), dma(4), dma(4), dma(4),
            *[dma(here * chunks) for _ in range(6)],
            dma(2), dma(2), dma(4), dma(4), dma(half_n - 1), dma(half_n - 1),
            dma(n_region - 1), dma(n_region - 1), dma(6), dma(6), dma(3), dma(3),
        ],
        compiler_params=pltpu.CompilerParams(
            collective_id=0, has_side_effects=True, vmem_limit_bytes=60 * 2**20
        ),
    )(
        latent, w_node, bias.reshape(1, width), w_out, edge_src.T, edge_weight.T, target,
        area.reshape(1, points),
    )
    grad_node, grad_out, grad_bias, loss = pl.pallas_call(
        functools.partial(widen, variables, vp),
        out_shape=(
            jax.ShapeDtypeStruct((rb, width), F32),
            jax.ShapeDtypeStruct((variables, width), F32),
            jax.ShapeDtypeStruct((1, width), F32),
            jax.ShapeDtypeStruct((1,), F32),
        ),
        in_specs=[pl.BlockSpec(memory_space=pltpu.VMEM)] * 3,
        out_specs=[pl.BlockSpec(memory_space=pltpu.VMEM)] * 3
        + [pl.BlockSpec(memory_space=pltpu.SMEM)],
    )(node_half, head_half, loss_sum)
    return (grad_node, grad_out, grad_bias.reshape(width), loss)


def solution(mesh):
    return jax.shard_map(
        functools.partial(local, mesh.shape["member"], mesh.shape["region"]),
        mesh=mesh,
        in_specs=(
            P("member", "region", None),
            P(),
            P(),
            P(),
            P("region", None),
            P("region", None),
            P(None, "region"),
            P("region"),
        ),
        out_specs=(P("region", None), P(), P(), P("region")),
        check_vma=False,
    )
```

```python
import functools

import jax
import jax.numpy as jnp
from jax import lax
from jax.experimental import pallas as pl
from jax.experimental.pallas import tpu as pltpu
from jax.sharding import PartitionSpec as P

smooth_sq = 0.01
gelu_c = 0.7978845608028654
gelu_a = 0.044715
MESH = pl.DeviceIdType.MESH
BF = jnp.bfloat16
F32 = jnp.float32


def decoder(
    n_member, n_region, variables,
    latent, w_node, bias, w_out_in, src_t, weight_t, target, area,
    node_out, head_out, loss_out,
    w_out, tail, ext, proj, adj, adj_t, hid, slope, preds, dpr, acc, gout, lacc, cb,
    part, recv_c, sum_c, recv_1a, recv_1b, sum_1a, sum_1b, recv_2, sum_2, recv_z, ob, lbuf,
    halo_s, halo_r, relay_s, relay_r, pa_s, pa_r, pb_s, pb_r, pf_s, pf_r,
    c_s, c_r, red_s, red_r, z_s, z_r, h_s, h_r, o_s, o_r, l_s, l_r,
):
    here, nodes, width = latent.shape
    fanout, points = src_t.shape
    span = 3 * nodes
    vp = w_out.shape[0]
    chunks, wide, gc = adj_t.shape
    rb = width // n_region
    quarter = width // 4
    half_n = n_region // 2
    count = here * n_member
    m = lax.axis_index("member")
    r = lax.axis_index("region")
    core = m % 2
    yy = m // 2
    xx = r % 2
    zz = r // 2
    m_core = m + 1 - 2 * core
    m_y = (1 - yy) * 2 + core
    m_diag = (1 - yy) * 2 + 1 - core
    r_x = r + 1 - 2 * xx
    r_relay = (r + n_region + 2 - 4 * xx) % n_region

    def remote(a, b, s, t, mm, rr):
        return pltpu.make_async_remote_copy(
            src_ref=a, dst_ref=b, send_sem=s, recv_sem=t, device_id=(mm, rr), device_id_type=MESH
        )

    barrier = pltpu.get_barrier_semaphore()
    for mm in (m_core, m_y, m_diag):
        pl.semaphore_signal(barrier, inc=1, device_id=(mm, r), device_id_type=MESH)
    for k in range(1, n_region):
        pl.semaphore_signal(
            barrier, inc=1, device_id=(m, (r + k) % n_region), device_id_type=MESH
        )
    pl.semaphore_wait(barrier, n_region + 2)

    far = 2 * xx
    near = 2 - far
    pieces = [(a, b) for a in range(here) for b in range(2)]
    hn = nodes // 2

    def halo(i):
        a, b = pieces[i]
        rows = pl.ds(b * hn, hn)
        return remote(
            latent.at[a, rows], ext.at[far, a, rows], halo_s.at[i], halo_r.at[i], m, r_x
        )

    def relay(i):
        a, b = pieces[i]
        rows = pl.ds(b * hn, hn)
        return remote(
            ext.at[near, a, rows], ext.at[far, a, rows], relay_s.at[i], relay_r.at[i], m, r_relay
        )

    for i in range(len(pieces)):
        halo(i).start()

    def project(a):
        proj[a] = jnp.dot(
            ext[:, a].reshape(span, width), w_node[...], preferred_element_type=F32
        ).astype(BF)

    ext[1] = latent[...]
    w_out[0:variables] = w_out_in[...]
    w_out[variables:vp] = jnp.zeros((vp - variables, width), BF)
    tail[...] = jnp.zeros_like(tail)
    tail[0 : variables - (vp - 16)] = target[vp - 16 : variables]

    def build(c, _):
        rows = pl.ds(pl.multiple_of(c * gc, gc), gc)
        row = lax.broadcasted_iota(jnp.int32, (span, gc), 0)
        st = src_t[:, rows]
        wt = weight_t[:, rows]
        at = jnp.zeros((span, gc), F32)
        for k in range(fanout):
            at = at + jnp.where(st[k : k + 1, :] == row, wt[k : k + 1, :], 0.0)
        adj[rows, :] = at.T.astype(BF)
        adj_t[c, 0:span, :] = at.astype(BF)
        adj_t[c, span:wide, :] = jnp.ones((wide - span, gc), BF)
        return 0

    lax.fori_loop(0, chunks // 4, build, 0)
    halo(0).wait_recv()
    relay(0).start()
    lax.fori_loop(chunks // 4, chunks, build, 0)
    halo(1).wait_recv()
    relay(1).start()
    relay(0).wait_recv()
    relay(1).wait_recv()

    lag = chunks // 2

    def blocks(t):
        return t // chunks, t % chunks

    def to_core(t):
        a, c = blocks(t)
        return remote(preds.at[0, a, c], preds.at[1, a, c], pa_s.at[t], pa_r.at[t], m_core, r)

    def to_y(t):
        a, c = blocks(t)
        return remote(preds.at[0, a, c], preds.at[2, a, c], pb_s.at[t], pb_r.at[t], m_y, r)

    def pass_on(t):
        a, c = blocks(t)
        return remote(preds.at[2, a, c], preds.at[3, a, c], pf_s.at[t], pf_r.at[t], m_core, r)

    steps = here * chunks

    def forward(a, c):
        rows = pl.ds(pl.multiple_of(c * gc, gc), gc)
        t = a * chunks + c
        x = jnp.dot(adj[rows, :], proj[a], preferred_element_type=F32) + bias[...]
        u = x * x
        th = jnp.tanh(x * (gelu_c + gelu_c * gelu_a * u))
        p = 0.5 + 0.5 * th
        h = x * p
        hb = h.astype(BF)
        hid[a, rows, :] = hb
        sl = p + h * (1.0 - p) * (2.0 * gelu_c + 6.0 * gelu_c * gelu_a * u)
        slope[a, rows, :] = sl.astype(BF)
        preds[0, a, c] = lax.dot_general(
            w_out[...], hb, (((1,), (1,)), ((), ())), preferred_element_type=F32
        ).astype(BF)
        to_y(t).start()
        to_core(t).start()

        @pl.when(t >= lag)
        def _():
            to_y(t - lag).wait_recv()
            pass_on(t - lag).start()

    for a in range(here):
        project(a)

        def run(c, _):
            if a + 1 < here:
                for b in range(2):
                    @pl.when(c == 2 * b)
                    def _():
                        halo(2 * a + 2 + b).wait_recv()
                        relay(2 * a + 2 + b).start()

            forward(a, c)
            return 0

        lax.fori_loop(0, chunks, run, 0)
        if a + 1 < here:
            for b in range(2):
                relay(2 * a + 2 + b).wait_recv()

    acc[...] = jnp.zeros_like(acc)
    gout[...] = jnp.zeros_like(gout)
    lacc[...] = jnp.zeros_like(lacc)
    step = 16

    def backward(c, _):
        rows = pl.ds(pl.multiple_of(c * gc, gc), gc)

        for a in range(here):
            to_core(a * chunks + c).wait_recv()
            pass_on(a * chunks + c).wait_recv()
        arow = area[:, rows]
        ascale = arow * (1.0 / variables)
        for v in range(0, vp, step):
            vs = slice(v, v + step)
            ps = [preds[s, a, c, vs, :].astype(F32) for s in range(4) for a in range(here)]
            tg = target[vs, rows] if v + step <= variables else tail[:, rows]
            dist = jnp.zeros((step, gc), F32)
            sums = [jnp.zeros((step, gc), F32) for _ in range(here)]
            for a in range(here):
                for b in range(a + 1, count):
                    d = ps[a] - ps[b]
                    q = d * d + smooth_sq
                    i = lax.rsqrt(q)
                    g = d * i
                    sums[a] = sums[a] + g
                    s = q * i
                    if b < here:
                        sums[b] = sums[b] - g
                        s = s + s
                    dist = dist + s
            total = dist * (-1.0 / (2.0 * count * (count - 1)))
            for a in range(here):
                e = ps[a] - tg
                q = e * e + smooth_sq
                i = lax.rsqrt(q)
                total = total + q * i * (1.0 / count)
                br = e * i * (1.0 / count) - sums[a] * (1.0 / (count * (count - 1)))
                dpr[a, vs, :] = (br * ascale).astype(BF)
            total = total * arow
            if v + step > variables:
                keep = lax.broadcasted_iota(jnp.int32, (step, gc), 0) < variables - v
                total = jnp.where(keep, total, 0.0)
            lacc[...] += total
        for a in range(here):
            dp = dpr[a]
            hb = hid[a, rows, :]
            gout[0:vp] += jnp.dot(dp, hb, preferred_element_type=F32)
            dh = lax.dot_general(
                dp, w_out[...], (((0,), (0,)), ((), ())), preferred_element_type=F32
            )
            dpre = (dh * slope[a, rows, :].astype(F32)).astype(BF)
            acc[a] += jnp.dot(adj_t[c], dpre, preferred_element_type=F32)

        @pl.when(c < lag)
        def _():
            to_y(steps - lag + c).wait_recv()
            pass_on(steps - lag + c).start()

        return 0

    lax.fori_loop(0, chunks, backward, 0)

    lbuf[0] = jnp.broadcast_to(
        jnp.sum(lacc[...]) * (1.0 / (variables * points)), lbuf.shape[1:]
    )

    def share_loss(k, mm):
        return remote(lbuf.at[0], lbuf.at[k], l_s.at[k - 1], l_r.at[k - 1], mm, r)

    sharing = [share_loss(k + 1, mm) for k, mm in enumerate((m_core, m_y, m_diag))]
    for copy in sharing:
        copy.start()

    bias_row = acc[0, span : span + 1, :]
    for a in range(1, here):
        bias_row = bias_row + acc[a, span : span + 1, :]
    gout[vp : vp + 1] = bias_row
    for a in range(here):
        for s in range(3):
            cb[s * here + a] = acc[a, s * nodes : (s + 1) * nodes, :].astype(BF)

    def add(a, b):
        return a.astype(F32) + b.astype(F32)

    c_copies = [
        remote(part.at[0, k], recv_c.at[k], c_s.at[k], c_r.at[k], m_core, r) for k in range(2)
    ]
    tall = 256
    lanes = quarter // 2
    for hh, side in enumerate((1 - core, core)):
        cols = pl.ds(pl.multiple_of(side * 2 * quarter, 2 * quarter), 2 * quarter)
        right = cb[:, :, cols].reshape(span * here, 2 * quarter)
        for i in range(0, width, tall):
            left = ext[:, :, :, i : i + tall].reshape(span * here, tall)
            g = lax.dot_general(
                left, right, (((0,), (0,)), ((), ())), preferred_element_type=F32
            ).astype(BF)
            for j in range(tall // rb):
                q = i // rb + j
                for k in range(4):
                    part[hh, k % 2, k // 2, q % 2, q // 2, 0:rb, :] = g[
                        j * rb : (j + 1) * rb, k * lanes : (k + 1) * lanes
                    ]
        for q in range(n_region):
            hv = gout[16 * q : 16 * q + 16, cols].astype(BF)
            for k in range(4):
                part[hh, k % 2, k // 2, q % 2, q // 2, rb : rb + 16, :] = hv[
                    :, k * lanes : (k + 1) * lanes
                ]
        if hh == 0:
            for copy in c_copies:
                copy.start()

    def add_c(k):
        def body(i, _):
            for a in range(2):
                for b in range(2):
                    sum_c[k, a, b, i] = add(part[1, k, a, b, i], recv_c[k, a, b, i]).astype(BF)
            return 0

        lax.fori_loop(0, half_n, body, 0)

    a1 = remote(sum_c.at[0, 1 - yy], recv_1a, red_s.at[0], red_r.at[0], m_y, r)
    b1 = remote(sum_c.at[1, :, 1 - xx], recv_1b, red_s.at[1], red_r.at[1], m, r_x)
    a2 = remote(sum_1a.at[1 - xx], recv_2.at[0], red_s.at[2], red_r.at[2], m, r_x)
    b2 = remote(sum_1b.at[1 - yy], recv_2.at[1], red_s.at[3], red_r.at[3], m_y, r)
    for k, copy in enumerate((a1, b1)):
        c_copies[k].wait_recv()
        add_c(k)
        copy.start()

    def add_1a(i, _):
        for b in range(2):
            sum_1a[b, i] = add(sum_c[0, yy, b, i], recv_1a[b, i]).astype(BF)
        return 0

    def add_1b(i, _):
        for b in range(2):
            sum_1b[b, i] = add(sum_c[1, b, xx, i], recv_1b[b, i]).astype(BF)
        return 0

    a1.wait_recv()
    lax.fori_loop(0, half_n, add_1a, 0)
    a2.start()
    b1.wait_recv()
    lax.fori_loop(0, half_n, add_1b, 0)
    b2.start()

    def add_2a(i, _):
        sum_2[i, 0] = add(sum_1a[xx, i], recv_2[0, i]).astype(BF)
        return 0

    def add_2b(i, _):
        sum_2[i, 1] = add(sum_1b[yy, i], recv_2[1, i]).astype(BF)
        return 0

    a2.wait_recv()
    lax.fori_loop(0, half_n, add_2a, 0)
    b2.wait_recv()
    lax.fori_loop(0, half_n, add_2b, 0)
    z_copies = []
    for k in range(1, half_n):
        z_to = (zz + k) % half_n
        z_copies.append(
            remote(
                sum_2.at[z_to], recv_z.at[k - 1], z_s.at[k - 1], z_r.at[k - 1], m, 2 * z_to + xx
            )
        )
    for copy in z_copies:
        copy.start()
    mine = pl.ds(pl.multiple_of(rb + 16 * r, 16), 16)
    totals = [sum_2[zz, k].astype(F32) for k in range(2)]
    for i in range(1, half_n):
        z_copies[i - 1].wait_recv()
        for k in range(2):
            totals[k] = totals[k] + recv_z[i - 1, k].astype(F32)
    for k in range(2):
        at = slice(k * lanes, (k + 1) * lanes)
        ob[0, 0:rb, at] = totals[k][0:rb].astype(BF)
        ob[0, mine, at] = totals[k][rb : rb + 16].astype(BF)
    h_copies = [
        remote(
            ob.at[0, mine], ob.at[0, mine], h_s.at[k - 1], h_r.at[k - 1], m, (r + k) % n_region
        )
        for k in range(1, n_region)
    ]
    for copy in h_copies:
        copy.start()
    tops, lows = pl.ds(0, rb), pl.ds(rb, 16 * n_region)

    def spread(rows, k):
        one = remote(ob.at[0, rows], ob.at[1, rows], o_s.at[k], o_r.at[k], m_core, r)
        two = remote(ob.at[0, rows], ob.at[2, rows], o_s.at[k + 1], o_r.at[k + 1], m_y, r)
        on = remote(ob.at[2, rows], ob.at[3, rows], o_s.at[k + 2], o_r.at[k + 2], m_core, r)
        return one, two, on

    t_core, t_y, t_on = spread(tops, 0)
    b_core, b_y, b_on = spread(lows, 3)
    t_y.start()
    t_core.start()

    def columns(mm):
        return pl.ds(pl.multiple_of(((mm % 2) * 2 + mm // 2) * quarter, quarter), quarter)

    def place_top(k, mm):
        node_out[:, columns(mm)] = ob[k, 0:rb, :]

    def place_low(k, mm):
        head_out[:, columns(mm)] = ob[k, rb : rb + vp + 16, :]

    place_top(0, m)
    for copy in sharing:
        copy.wait_recv()
    loss_out[...] = (lbuf[0] + lbuf[1]) + (lbuf[2] + lbuf[3])
    for copy in h_copies:
        copy.wait_recv()
    b_y.start()
    b_core.start()
    t_y.wait_recv()
    t_on.start()
    place_top(2, m_y)
    t_core.wait_recv()
    place_top(1, m_core)
    place_low(0, m)
    b_y.wait_recv()
    b_on.start()
    place_low(2, m_y)
    b_core.wait_recv()
    place_low(1, m_core)
    t_on.wait_recv()
    place_top(3, m_diag)
    b_on.wait_recv()
    place_low(3, m_diag)

    for i in range(len(pieces)):
        halo(i).wait_send()
        relay(i).wait_send()

    def drain(c, _):
        to_core(c).wait_send()
        to_y(c).wait_send()
        pass_on(c).wait_send()
        return 0

    lax.fori_loop(0, steps, drain, 0)
    ends = [a1, b1, a2, b2, t_core, t_y, t_on, b_core, b_y, b_on]
    for copy in ends + c_copies + z_copies + h_copies + sharing:
        copy.wait_send()


def widen(variables, vp, node_half, head_half, loss_sum, grad_node, grad_out, grad_bias, loss):
    grad_node[...] = node_half[...].astype(F32)
    grad_out[...] = head_half[0:vp, :].astype(F32)[0:variables]
    grad_bias[...] = head_half[vp : vp + 16, :].astype(F32)[0:1]
    loss[0] = jnp.max(loss_sum[...])


def local(n_member, n_region, latent, w_node, bias, w_out, edge_src, edge_weight, target, area):
    here, nodes, width = latent.shape
    points, fanout = edge_src.shape
    variables = target.shape[0]
    vp = -(-variables // 16) * 16
    gc = 512
    chunks = points // gc
    span = 3 * nodes
    wide = span + 16
    rb = width // n_region
    head = 16 * n_region
    quarter = width // 4
    lanes = quarter // 2
    half_n = n_region // 2
    blk = rb + 16
    grow = max(head, vp + 16)
    dma = lambda k: pltpu.SemaphoreType.DMA((k,))
    vm = lambda shape, t: pltpu.VMEM(shape, t)
    node_half, head_half, loss_sum = pl.pallas_call(
        functools.partial(decoder, n_member, n_region, variables),
        out_shape=(
            jax.ShapeDtypeStruct((rb, width), BF),
            jax.ShapeDtypeStruct((vp + 16, width), BF),
            jax.ShapeDtypeStruct((8, 128), F32),
        ),
        in_specs=[pl.BlockSpec(memory_space=pltpu.VMEM)] * 8,
        out_specs=[pl.BlockSpec(memory_space=pltpu.VMEM)] * 3,
        scratch_shapes=[
            vm((vp, width), BF),
            vm((16, points), F32),
            vm((3, here, nodes, width), BF),
            vm((here, span, width), BF),
            vm((points, span), BF),
            vm((chunks, wide, gc), BF),
            vm((here, points, width), BF),
            vm((here, points, width), BF),
            vm((4, here, chunks, vp, gc), BF),
            vm((here, vp, gc), BF),
            vm((here, wide, width), F32),
            vm((grow, width), F32),
            vm((16, gc), F32),
            vm((3 * here, nodes, width), BF),
            vm((2, 2, 2, 2, half_n, blk, lanes), BF),
            vm((2, 2, 2, half_n, blk, lanes), BF),
            vm((2, 2, 2, half_n, blk, lanes), BF),
            vm((2, half_n, blk, lanes), BF),
            vm((2, half_n, blk, lanes), BF),
            vm((2, half_n, blk, lanes), BF),
            vm((2, half_n, blk, lanes), BF),
            vm((2, half_n, blk, lanes), BF),
            vm((half_n, 2, blk, lanes), BF),
            vm((half_n - 1, 2, blk, lanes), BF),
            vm((4, rb + head, quarter), BF),
            vm((4, 8, 128), F32),
            dma(4), dma(4), dma(4), dma(4),
            *[dma(here * chunks) for _ in range(6)],
            dma(2), dma(2), dma(4), dma(4), dma(half_n - 1), dma(half_n - 1),
            dma(n_region - 1), dma(n_region - 1), dma(6), dma(6), dma(3), dma(3),
        ],
        compiler_params=pltpu.CompilerParams(
            collective_id=0, has_side_effects=True, vmem_limit_bytes=60 * 2**20
        ),
    )(
        latent, w_node, bias.reshape(1, width), w_out, edge_src.T, edge_weight.T, target,
        area.reshape(1, points),
    )
    grad_node, grad_out, grad_bias, loss = pl.pallas_call(
        functools.partial(widen, variables, vp),
        out_shape=(
            jax.ShapeDtypeStruct((rb, width), F32),
            jax.ShapeDtypeStruct((variables, width), F32),
            jax.ShapeDtypeStruct((1, width), F32),
            jax.ShapeDtypeStruct((1,), F32),
        ),
        in_specs=[pl.BlockSpec(memory_space=pltpu.VMEM)] * 3,
        out_specs=[pl.BlockSpec(memory_space=pltpu.VMEM)] * 3
        + [pl.BlockSpec(memory_space=pltpu.SMEM)],
    )(node_half, head_half, loss_sum)
    return (grad_node, grad_out, grad_bias.reshape(width), loss)


def solution(mesh):
    return jax.shard_map(
        functools.partial(local, mesh.shape["member"], mesh.shape["region"]),
        mesh=mesh,
        in_specs=(
            P("member", "region", None),
            P(),
            P(),
            P(),
            P("region", None),
            P("region", None),
            P(None, "region"),
            P("region"),
        ),
        out_specs=(P("region", None), P(), P(), P("region")),
        check_vma=False,
    )
```
